32 devices in a mesh: wave: 4 (over z), tile: 8 (over y, x, core).
Axes of the slice: x: 2, y: 2, z: 4, core: 2. Of those that a mesh axis runs over, the one named last changes fastest.
Arguments:
- hit_energy: bfloat16 [1024, 32, 128], P('tile', 'wave'), may hold values from -24 to 24
- hit_spot: int32 [4, 1024, 128], P('wave', 'tile'), may hold values from 0 to 511
- block_tile: int32 [4, 1024, 1], P('wave', 'tile'), may hold values from 0 to 7; in each aligned block of 128 rows (0 to 127, 128 to 255, ..., all dimensions but the last counted through in order) at most 32 rows name the same one
- block_count: int32 [4, 1024], P('wave', 'tile'), may hold values from 64 to 128
- block_scene: int32 [4, 1024], P('wave', 'tile'), may hold values from 0 to 3
- block_row: int32 [4, 1024], P('wave', 'tile'), may hold values from 0 to 12
- psf_bank: float32 [64, 32, 961], P(None, 'wave'), may hold values from 0 to 0.004162331
- psf_index: int32 [8, 4, 1], P('tile'), may hold values from 0 to 63
- response: float32 [32, 3], replicated, may hold values from -1 to 1
- conv_in: bfloat16 [64, 3, 3, 3], replicated, may hold values from -1.25 to 1.25
- conv_out: bfloat16 [64, 64, 3, 3], replicated, may hold values from -0.25 to 0.25
Outputs:
- features: bfloat16 [4, 64, 128, 128], P('wave', None, 'tile')
The draws below stay inside these ranges and needn't reach their ends.
Inputs may be any that keep to these rules, and one draw needn't show every extreme that they name: `block_tile`: among the 128 blocks of one device at most 32 name the same tile, a bound that some device reaches.
All inputs are finite; a program needn't handle non-finite values.
Results may differ from the reference program's by a relative error of at most 0.0058.
Values may be sent and summed in bfloat16 or wider, within the bound.
A program may use at most 64 MiB of HBM per device.

```python
import math
import jax
import jax.numpy as jnp
import numpy as np
from jax import lax

BAND_DEV = 8
BANDS = 32
HITS = 128
NB = 128
CAP = 32
BLOCKS = 1024
ROWS_DEV = 16
W = 128
H = 128
SCENES = 4
WIN = 4
K = 31
PW = 128
PATCHES = 1
NPSF = 64
CH = 64
N_WAVE = 4
N_TILE = 8


def touch_ends(result, rng, smallest, largest):
    shape = result.shape
    index_at = [jax.random.randint(jax.random.fold_in(rng, axis), (), 0, shape[axis]) for axis in range(len(shape))]
    result = result.at[tuple(index_at)].set(smallest)
    longest = shape.index(max(shape))
    index_at[longest] = (index_at[longest] + 1) % shape[longest]
    return result.at[tuple(index_at)].set(largest)


def block_scale(key, dims, cuts, least, largest):
    loudness = 1.0
    for axis_at, parts in cuts:
        heights = jax.random.uniform(jax.random.fold_in(jax.random.fold_in(key, 6), axis_at), (parts,), jnp.float32, least / len(cuts), largest / len(cuts))
        loudness = loudness * jnp.repeat(jnp.exp(heights), dims[axis_at] // parts).reshape((-1,) + (1,) * (len(dims) - 1 - axis_at))
    return loudness


def deal_out(key, own, number, rows, amount, top, bound, lean):
    order = jax.random.permutation(key, amount)
    crowded, usual = shares(amount, rows * top, bound, lean, True), shares(amount, rows * top, bound, lean, False)
    places = jnp.arange(amount)

    def named(lengths, turn):
        used = int((lengths > 0).sum())
        fixed = max(1, used // 4)
        passed = fixed + (places - fixed + turn * (used - fixed)) % max(1, amount - fixed)
        return jnp.zeros((amount,), jnp.int32).at[order[jnp.where(places < fixed, places, passed)]].set(jnp.asarray(lengths, jnp.int32))

    lengths = jnp.where(number % 4 == 0, named(crowded, number // 4), named(usual, number - number // 4 - 1))
    mixed = jax.random.permutation(jax.random.fold_in(own, 3), amount)
    giver, taker = mixed[0:amount // 2 * 2:2], mixed[1:amount // 2 * 2:2]
    slack = jnp.minimum(lengths[giver] - 1, bound - lengths[taker]) // 2
    slack = jnp.where((giver == order[0]) | (taker == order[0]) | (lengths[taker] == 0), 0, jnp.maximum(slack, 0))
    passed = jax.random.randint(jax.random.fold_in(own, 4), (amount // 2,), 0, 1 << 20) % (slack + 1)
    lengths = lengths.at[giver].add(-passed).at[taker].add(passed)
    members = jnp.searchsorted(jnp.cumsum(lengths), jnp.arange(rows * top), side="right").astype(jnp.int32)
    grid = members.reshape(top, rows).T
    grid = grid[jax.random.permutation(jax.random.fold_in(own, 1), rows)]
    turn = jax.random.randint(jax.random.fold_in(own, 2), (rows, 1), 0, top)
    return jnp.take_along_axis(grid, (jnp.arange(top)[None, :] + turn) % top, axis=1)


def shares(number_of, total, bound, skew, full):
    weights = [(1 << 20) // math.isqrt(standing ** skew) + 1 for standing in range(1, number_of + 1)]
    largest = bound if full else min(bound, max(-(-total // number_of), total * weights[0] // sum(weights)))
    least = 1 if total - largest >= number_of - 1 else 0
    holding, rest = [largest] + [least] * (number_of - 1), total - largest - least * (number_of - 1)
    while rest > 0:
        movable = [i for i in range(1, number_of) if holding[i] < largest] or [i for i in range(1, number_of) if holding[i] < bound]
        mass, left = sum([weights[i] for i in movable]), rest
        for i in movable:
            addition = min(bound - holding[i], max(1, left * weights[i] // mass), rest)
            holding[i] = holding[i] + addition
            rest = rest - addition
    return np.array(holding)


def gaussian(key, dims, deviation, bound, shards=(), kind=jnp.bfloat16):
    drawn = deviation * jax.random.normal(key, dims, jnp.float32)
    if shards:
        drawn = drawn * block_scale(key, dims, shards, -0.22, 0.18)
    return jnp.clip(drawn, -bound, bound).astype(kind)


def setup_inputs(seed: int = 0) -> dict:
    keys = jax.random.split(jax.random.key(seed), 12)
    hit_energy = gaussian(keys[0], (BLOCKS, BANDS, HITS), 4.0, 24.0, ((0, 8), (1, 4)))
    hit_spot = touch_ends(jax.random.randint(keys[1], (N_WAVE, BLOCKS, HITS), 0, WIN * W), jax.random.fold_in(keys[1], 1), 0, (WIN * W) - 1).astype(jnp.int32)
    block_tile_keys = jax.random.split(jax.random.fold_in(keys[2], 1), N_WAVE * BLOCKS // NB)
    block_tile_turns = jax.random.permutation(jax.random.fold_in(keys[2], 3), N_WAVE * BLOCKS // NB)
    block_tile = jax.vmap(lambda own, number: deal_out(jax.random.fold_in(keys[2], 2), own, number, NB, N_TILE, 1, CAP, 2))(block_tile_keys, block_tile_turns).reshape((N_WAVE, BLOCKS, 1))
    block_count = touch_ends(jax.random.randint(keys[3], (N_WAVE, BLOCKS), 64, 129), jax.random.fold_in(keys[3], 1), 64, 128).astype(jnp.int32)
    block_scene = touch_ends(jax.random.randint(keys[4], (N_WAVE, BLOCKS), 0, SCENES), jax.random.fold_in(keys[4], 1), 0, SCENES - 1).astype(jnp.int32)
    block_row = touch_ends(jax.random.randint(keys[5], (N_WAVE, BLOCKS), 0, ROWS_DEV - WIN + 1), jax.random.fold_in(keys[5], 1), 0, ROWS_DEV - WIN).astype(jnp.int32)
    psf_bank = jnp.clip(0.004162331 * jax.random.uniform(keys[6], (NPSF, BANDS, K * K), jnp.float32) ** block_scale(keys[6], (NPSF, BANDS, K * K), ((1, 4),), -0.2, 0.2), 0.0, 0.004162331)
    psf_index = touch_ends(jax.random.randint(keys[7], (N_TILE, SCENES, PATCHES), 0, NPSF), jax.random.fold_in(keys[7], 1), 0, NPSF - 1).astype(jnp.int32)
    response = gaussian(keys[8], (BANDS, 3), BANDS ** -0.5, 1.0, (), jnp.float32)
    conv_in = gaussian(keys[9], (CH, 3, 3, 3), 27 ** -0.5, 1.25)
    conv_out = gaussian(keys[10], (CH, CH, 3, 3), (9 * CH) ** -0.5, 0.25)
    return {"hit_energy": hit_energy, "hit_spot": hit_spot, "block_tile": block_tile, "block_count": block_count, "block_scene": block_scene, "block_row": block_row, "psf_bank": psf_bank, "psf_index": psf_index, "response": response, "conv_in": conv_in, "conv_out": conv_out}


def convolve(image, weights):
    return lax.conv_general_dilated(image.astype(jnp.float32), weights.astype(jnp.float32), (1, 1), ((1, 1), (1, 1)), dimension_numbers=("NCHW", "OIHW", "NCHW"), precision=lax.Precision.HIGHEST)


def reference(hit_energy, hit_spot, block_tile, block_count, block_scene, block_row, psf_bank, psf_index, response, conv_in, conv_out):
    radius = K // 2
    lanes = jnp.arange(HITS, dtype=jnp.int32)
    groups = []
    for group in range(N_WAVE):
        energy = hit_energy[:, group * BAND_DEV:(group + 1) * BAND_DEV, :]
        live = lanes[None, :] < block_count[group][:, None]
        masked = jnp.where(live[:, None, :], energy, jnp.zeros_like(energy)).astype(jnp.float32)
        row_top = block_tile[group, :, 0] * ROWS_DEV + block_row[group]
        flat = ((block_scene[group] * H + row_top) * W)[:, None] + hit_spot[group]
        image = jnp.zeros((BAND_DEV, SCENES * H * W), jnp.float32)
        image = image.at[:, flat.reshape(-1)].add(jnp.transpose(masked, (1, 0, 2)).reshape(BAND_DEV, -1))
        groups.append(image.reshape(BAND_DEV, SCENES, H, W))
    splat = jnp.concatenate(groups, axis=0)

    def one_scene(scene):
        plane = lax.dynamic_index_in_dim(splat, scene, 1, keepdims=False)
        padded = jnp.pad(plane, ((0, 0), (radius, radius), (radius, radius)))
        scene_index = lax.dynamic_index_in_dim(psf_index, scene, 1, keepdims=False)

        def one_tile(tile_number):
            strip = lax.dynamic_slice_in_dim(padded, (tile_number * ROWS_DEV).astype(jnp.int32), ROWS_DEV + 2 * radius, 1)
            pieces = jnp.stack([strip[:, :, column * PW:column * PW + PW + 2 * radius] for column in range(PATCHES)], axis=1)
            stacked = pieces.reshape(1, BANDS * PATCHES, ROWS_DEV + 2 * radius, PW + 2 * radius)
            chosen = psf_bank[lax.dynamic_index_in_dim(scene_index, tile_number, 0, keepdims=False)]
            kernels = jnp.transpose(chosen, (1, 0, 2)).reshape(BANDS * PATCHES, 1, K, K)
            out = lax.conv_general_dilated(stacked, kernels, (1, 1), "VALID", dimension_numbers=("NCHW", "OIHW", "NCHW"), feature_group_count=BANDS * PATCHES, precision=lax.Precision.HIGHEST)
            out = out.reshape(BANDS, PATCHES, ROWS_DEV, PW).transpose(0, 2, 1, 3)
            return out.reshape(BANDS, ROWS_DEV, W)

        strips = lax.map(one_tile, jnp.arange(N_TILE, dtype=jnp.int32))
        blurred = jnp.transpose(strips, (1, 0, 2, 3)).reshape(BANDS, H, W)
        color = jnp.einsum("byx,bc->cyx", blurred, response, precision=lax.Precision.HIGHEST)
        sensor = color.astype(jnp.bfloat16)
        hidden = jax.nn.silu(convolve(sensor[None], conv_in)).astype(jnp.bfloat16)
        return convolve(hidden, conv_out)[0].astype(jnp.bfloat16)

    return lax.map(one_scene, jnp.arange(SCENES, dtype=jnp.int32))
```

```python
import functools

import jax
import jax.numpy as jnp
from jax import lax
from jax.experimental import pallas as pl
from jax.experimental.pallas import tpu as pltpu
from jax.sharding import PartitionSpec as P

ROWS = 16
W = 128
WIN = 4
K = 31
RAD = K // 2
PITCH = 32
DEPTH = ROWS * PITCH
MESH = pl.DeviceIdType.MESH
F32 = jnp.float32
BF16 = jnp.bfloat16


def dispatch_kernel(n, cap, inv_ref, energy_ref, pos_ref, meta_ref, got_e, got_p, got_m,
                    out_e, out_p, send_sem, recv_sem, local_sem):
    wave = lax.axis_index("wave")
    me = lax.axis_index("tile")
    barrier = pltpu.get_barrier_semaphore()

    @pl.loop(1, n)
    def _(d):
        pl.semaphore_signal(barrier, inc=1, device_id=(wave, lax.rem(me + d, n)), device_id_type=MESH)

    def pack(peer):
        for j in range(cap):
            i = inv_ref[peer, j]
            out_e[peer, j] = energy_ref[jnp.minimum(i, energy_ref.shape[0] - 1)]
            out_p[peer, j] = pos_ref[i]

    def copies(d):
        peer = lax.rem(me + d, n)
        pairs = ((out_e.at[peer], got_e.at[me]), (out_p.at[peer], got_p.at[me]),
                 (meta_ref.at[peer], got_m.at[me]))
        return [
            pltpu.make_async_remote_copy(
                src_ref=src, dst_ref=dst, send_sem=send_sem.at[k, d], recv_sem=recv_sem.at[k, d],
                device_id=(wave, peer), device_id_type=MESH)
            for k, (src, dst) in enumerate(pairs)
        ]

    pack(lax.rem(me + 1, n))
    pl.semaphore_wait(barrier, n - 1)

    @pl.loop(1, n)
    def _(d):
        for copy in copies(d):
            copy.start()
        pack(lax.rem(me + d + 1, n))

    own = [pltpu.make_async_copy(src, dst, local_sem.at[k]) for k, (src, dst) in enumerate(
        ((out_e.at[me], got_e.at[me]), (out_p.at[me], got_p.at[me]), (meta_ref.at[me], got_m.at[me])))]
    for copy in own:
        copy.start()
    for copy in own:
        copy.wait()

    @pl.loop(1, n)
    def _(d):
        for copy in copies(d):
            copy.wait()


def dispatch(inv, energy, pos, meta):
    n, cap = inv.shape
    bands, lanes = energy.shape[1:]
    vmem = pl.BlockSpec(memory_space=pltpu.VMEM)
    hbm = pl.BlockSpec(memory_space=pl.ANY)
    return pl.pallas_call(
        functools.partial(dispatch_kernel, n, cap),
        out_shape=(
            jax.ShapeDtypeStruct((n, cap, bands, lanes), energy.dtype),
            jax.ShapeDtypeStruct((n, cap, 1, lanes), jnp.int32),
            jax.ShapeDtypeStruct((n, 1, lanes), jnp.int32),
        ),
        in_specs=[pl.BlockSpec(memory_space=pltpu.SMEM), vmem, vmem, vmem],
        out_specs=(hbm, hbm, hbm),
        scratch_shapes=[
            pltpu.VMEM((n, cap, bands, lanes), energy.dtype),
            pltpu.VMEM((n, cap, 1, lanes), jnp.int32),
            pltpu.SemaphoreType.DMA((3, n)),
            pltpu.SemaphoreType.DMA((3, n)),
            pltpu.SemaphoreType.DMA((3,)),
        ],
        compiler_params=pltpu.CompilerParams(
            collective_id=0, has_side_effects=True, vmem_limit_bytes=32 * 2**20),
        name="dispatch",
    )(inv, energy, pos, meta)


def blur_kernel(n, cap, scenes, bands, meta_ref, resp_ref, energy_ref, pos_ref, bank_ref, out_ref,
                acc, kpad, amat):
    me = lax.axis_index("tile")
    wave = lax.axis_index("wave")
    group = 8
    acc[...] = jnp.zeros_like(acc)
    xs = lax.broadcasted_iota(jnp.int32, (W, W), 0)

    def splat_source(d, carry):
        @pl.loop(0, cap // group)
        def _(g):
            windows = []
            for k in range(group):
                j = g * group + k
                pos = pos_ref[d, j]
                row = lax.shift_right_arithmetic(pos, 7)
                col = (W - 1) - (pos & (W - 1))
                onehot = jnp.where(xs == col, 1.0, 0.0).astype(BF16)
                energy = energy_ref[d, j].astype(F32)
                parts = [jnp.where(row == r, energy, 0.0) for r in range(WIN)]
                lhs = jnp.concatenate(parts, axis=0).astype(BF16)
                windows.append(lax.dot_general(
                    lhs, onehot, (((1,), (1,)), ((), ())), preferred_element_type=F32))
            for k in range(group):
                base = pl.multiple_of(meta_ref[d, g * group + k] * bands, bands)
                acc[pl.ds(base, WIN * bands), :] += windows[k]
        return carry

    lax.fori_loop(0, n, splat_source, 0)

    lane = lax.broadcasted_iota(jnp.int32, (bands, W), 1)
    shift_v = lax.broadcasted_iota(jnp.int32, (PITCH, W), 0)
    from_x = lax.broadcasted_iota(jnp.int32, (PITCH, W), 1) - shift_v + RAD
    keep = (from_x >= 0) & (from_x < W) & (shift_v < K)
    kpad[...] = jnp.zeros_like(kpad)

    def scene_step(s, carry):
        for part in range(3):
            other = jnp.clip(me + part - 1, 0, n - 1)
            flat = bank_ref[meta_ref[other, 64 + s]]
            flat = jnp.concatenate([flat, jnp.zeros((bands, 1024 + W - K * K), F32)], axis=1)
            for g in range(8):
                cell = jnp.zeros((bands, W), F32)
                for q in range(4):
                    u = 4 * g + q
                    if u >= K:
                        continue
                    base = K * u // W * W
                    shift = (PITCH * q - (K * u - base)) % (2 * W)
                    piece = flat[:, base:base + 2 * W]
                    if shift:
                        piece = pltpu.roll(piece, shift, 1)
                    hit = (lane >= PITCH * q) & (lane < PITCH * q + K)
                    cell = jnp.where(hit, piece[:, :W], cell)
                kpad[:, 512 + g * W:512 + (g + 1) * W] = cell
            for j in range(ROWS):
                start = 512 + PITCH * (RAD - j + ROWS * (1 - part))
                base = start // W * W
                off = start - base
                piece = kpad[:, base:base + DEPTH + W]
                if off:
                    piece = pltpu.roll(piece, DEPTH + W - off, 1)
                for c4 in range(DEPTH // W):
                    amat[c4, pl.ds(part * ROWS + j, bands, stride=3 * ROWS), :] = (
                        piece[:, c4 * W:(c4 + 1) * W])
        colours = [jnp.zeros((3 * ROWS, W), F32) for _ in range(3)]
        for b in range(bands):
            lhs = jnp.concatenate(
                [amat[c4, b * 3 * ROWS:(b + 1) * 3 * ROWS, :] for c4 in range(DEPTH // W)], axis=1
            ).astype(BF16)
            rows = []
            for r in range(ROWS):
                line = acc[pl.ds((s * ROWS + r) * bands + b, 1), :]
                wide = jnp.broadcast_to(line, (PITCH, W))
                wide = pltpu.roll(wide, W - RAD, 1, stride=1, stride_axis=0)
                rows.append(jnp.where(keep, wide, 0.0).astype(BF16))
            rhs = jnp.concatenate(rows, axis=0)
            blurred = jnp.dot(lhs, rhs, preferred_element_type=F32)
            for c in range(3):
                colours[c] = colours[c] + resp_ref[wave * bands + b, c] * blurred
        for part in range(3):
            for c in range(3):
                out_ref[s, part, c] = colours[c][part * ROWS:(part + 1) * ROWS]
        return carry

    lax.fori_loop(0, scenes, scene_step, 0)


def blur(meta, response, energy, pos, bank, scenes):
    n, cap, bands, lanes = energy.shape
    vmem = pl.BlockSpec(memory_space=pltpu.VMEM)
    smem = pl.BlockSpec(memory_space=pltpu.SMEM)
    return pl.pallas_call(
        functools.partial(blur_kernel, n, cap, scenes, bands),
        out_shape=jax.ShapeDtypeStruct((scenes, 3, 3, ROWS, W), F32),
        in_specs=[smem, smem, vmem, vmem, vmem],
        out_specs=vmem,
        scratch_shapes=[
            pltpu.VMEM((scenes * ROWS * bands, W), F32),
            pltpu.VMEM((bands, 2176), F32),
            pltpu.VMEM((DEPTH // W, bands * 3 * ROWS, W), F32),
        ],
        compiler_params=pltpu.CompilerParams(vmem_limit_bytes=48 * 2**20),
        name="blur",
    )(meta, response, energy, pos, bank)


def finish_kernel(waves, n, col_ref, w1_ref, w2_ref, out_ref, got, mine, rim, sens, hid, outs,
                  send_sem, recv_sem, rim_send, rim_recv):
    wave = lax.axis_index("wave")
    me = lax.axis_index("tile")
    has_up = me > 0
    has_down = me < n - 1
    barrier = pltpu.get_barrier_semaphore()

    def guarded(part, body):
        if part == 0:
            pl.when(has_up)(body)
        elif part == 2:
            pl.when(has_down)(body)
        else:
            body()

    todo = [(dw, part) for dw in range(waves) for part in range(3) if (dw, part) != (0, 1)]
    for dw, part in todo:
        def greet(dw=dw, part=part):
            pl.semaphore_signal(barrier, inc=1,
                                device_id=(lax.rem(wave + dw, waves), me + part - 1), device_id_type=MESH)
        guarded(part, greet)
    sides = jnp.where(has_up, 1, 0) + jnp.where(has_down, 1, 0)
    pl.semaphore_wait(barrier, waves - 1 + waves * sides)

    def copy_of(dw, part):
        scene = lax.rem(wave + dw, waves)
        return pltpu.make_async_remote_copy(
            src_ref=col_ref.at[scene, part], dst_ref=got.at[dw, part],
            send_sem=send_sem.at[dw, part], recv_sem=recv_sem.at[dw, part],
            device_id=(scene, me + part - 1), device_id_type=MESH)

    for dw, part in todo:
        guarded(part, lambda dw=dw, part=part: copy_of(dw, part).start())

    @pl.when(jnp.logical_not(has_down))
    def _():
        for dw in range(waves):
            got[dw, 0] = jnp.zeros(got.shape[2:], F32)
        rim[1] = jnp.zeros(rim.shape[1:], F32)

    @pl.when(jnp.logical_not(has_up))
    def _():
        for dw in range(waves):
            got[dw, 2] = jnp.zeros(got.shape[2:], F32)
        rim[0] = jnp.zeros(rim.shape[1:], F32)

    for dw, part in todo:
        guarded(2 - part, lambda dw=dw, part=part: copy_of(dw, part).wait_recv())
    total = col_ref[wave, 1]
    for dw, part in todo:
        total = total + got[dw, part]
    sensor = total.astype(BF16)
    flip_r = lax.broadcasted_iota(jnp.int32, (W, W), 0)
    flip_c = lax.broadcasted_iota(jnp.int32, (W, W), 1)
    mirror = jnp.where(flip_r + flip_c == W - 1, 1.0, 0.0).astype(BF16)
    plain = jnp.dot(sensor.reshape(3 * ROWS, W), mirror, preferred_element_type=F32)
    mine[...] = plain.reshape(3, ROWS, W)

    def to_down():
        return pltpu.make_async_remote_copy(
            src_ref=mine.at[:, pl.ds(8, 8)], dst_ref=rim.at[0], send_sem=rim_send.at[0],
            recv_sem=rim_recv.at[0], device_id=(wave, me + 1), device_id_type=MESH)

    def to_up():
        return pltpu.make_async_remote_copy(
            src_ref=mine.at[:, pl.ds(0, 8)], dst_ref=rim.at[1], send_sem=rim_send.at[1],
            recv_sem=rim_recv.at[1], device_id=(wave, me - 1), device_id_type=MESH)

    pl.when(has_down)(lambda: to_down().start())
    pl.when(has_up)(lambda: to_up().start())

    sens[...] = jnp.zeros_like(sens)
    for c in range(3):
        sens[pl.ds(2 * 8 + c, ROWS, stride=8), :] = plain[c * ROWS:(c + 1) * ROWS]
    pl.when(has_up)(lambda: to_down().wait_recv())
    pl.when(has_down)(lambda: to_up().wait_recv())
    for c in range(3):
        for k in range(2):
            sens[pl.ds(k * 8 + c, 1), :] = rim[0, c, 6 + k:7 + k]
            sens[pl.ds((ROWS + 2 + k) * 8 + c, 1), :] = rim[1, c, k:k + 1]

    def shifted(values):
        xs = lax.broadcasted_iota(jnp.int32, values.shape, 1)
        left = jnp.where(xs == 0, 0.0, pltpu.roll(values, 1, 1))
        right = jnp.where(xs == W - 1, 0.0, pltpu.roll(values, W - 1, 1))
        return left, values, right

    spread = jnp.concatenate(
        [jnp.concatenate(shifted(sens[y * 8:(y + 1) * 8, :]), axis=0) for y in range(ROWS + 4)], axis=0
    )
    w1 = w1_ref[...]
    for y in range(ROWS + 2):
        rhs = spread[y * 24:(y + 3) * 24].astype(BF16)
        value = jnp.dot(w1, rhs, preferred_element_type=F32)
        value = value / (1.0 + jnp.exp(-value))
        if y == 0:
            value = jnp.where(has_up, value, 0.0)
        if y == ROWS + 1:
            value = jnp.where(has_down, value, 0.0)
        hid[y] = jnp.concatenate(shifted(value), axis=0).astype(BF16)
    w2 = w2_ref[...]
    channels = w2.shape[0]
    for y in range(ROWS):
        rhs = hid[y:y + 3].reshape(9 * channels, W)
        outs[pl.ds(y, channels, stride=ROWS), :] = jnp.dot(w2, rhs, preferred_element_type=F32)
    out_ref[0] = outs[...].reshape(channels, ROWS, W).astype(BF16)

    for dw, part in todo:
        guarded(part, lambda dw=dw, part=part: copy_of(dw, part).wait_send())
    pl.when(has_down)(lambda: to_down().wait_send())
    pl.when(has_up)(lambda: to_up().wait_send())


def finish(col, w1, w2, waves, n):
    channels = w2.shape[0]
    vmem = pl.BlockSpec(memory_space=pltpu.VMEM)
    return pl.pallas_call(
        functools.partial(finish_kernel, waves, n),
        out_shape=jax.ShapeDtypeStruct((1, channels, ROWS, W), BF16),
        in_specs=[vmem] * 3,
        out_specs=vmem,
        scratch_shapes=[
            pltpu.VMEM((waves, 3, 3, ROWS, W), F32),
            pltpu.VMEM((3, ROWS, W), F32),
            pltpu.VMEM((2, 3, 8, W), F32),
            pltpu.VMEM(((ROWS + 4) * 8, W), F32),
            pltpu.VMEM((ROWS + 2, 3 * channels, W), BF16),
            pltpu.VMEM((channels * ROWS, W), F32),
            pltpu.SemaphoreType.DMA((waves, 3)),
            pltpu.SemaphoreType.DMA((waves, 3)),
            pltpu.SemaphoreType.DMA((2,)),
            pltpu.SemaphoreType.DMA((2,)),
        ],
        compiler_params=pltpu.CompilerParams(
            collective_id=1, has_side_effects=True, vmem_limit_bytes=32 * 2**20),
        name="finish",
    )(col, w1, w2)


def per_device(hit_energy, hit_spot, block_tile, block_count, block_scene, block_row, psf_bank,
               psf_index, response, conv_in, conv_out):
    n = lax.axis_size("tile")
    waves = lax.axis_size("wave")
    blocks, bands, lanes = hit_energy.shape
    cap = 2 * blocks // n
    scenes = psf_index.shape[1]
    target = block_tile[0, :, 0]
    base = block_scene[0] * ROWS + block_row[0]
    order = jnp.arange(blocks, dtype=jnp.int32)
    same = (target[:, None] == target[None, :]) & (order[None, :] < order[:, None])
    rank = jnp.sum(same.astype(jnp.int32), axis=1)
    tiles = jnp.arange(n, dtype=jnp.int32)
    slots = jnp.arange(lanes, dtype=jnp.int32)
    here = (target[None, None, :] == tiles[:, None, None]) & (rank[None, None, :] == slots[None, :, None])
    inv = blocks + jnp.sum(jnp.where(here, order - blocks, 0), axis=2)
    bases = jnp.sum(jnp.where(here, base, 0), axis=2)
    psf_row = jnp.pad(psf_index[0, :, 0], (64, lanes - 64 - scenes))
    meta = jnp.where(slots[None, :] < 64, bases, psf_row[None, :])[:, None, :]
    live = slots[None, :] < block_count[0][:, None]
    pos = jnp.where(live, hit_spot[0], -1)
    pos = jnp.concatenate([pos, jnp.full((1, lanes), -1, jnp.int32)], axis=0)[:, None, :]
    got_e, got_p, got_m = dispatch(inv[:, :cap], hit_energy, pos, meta)
    col = blur(got_m[:, 0, :], response, got_e, got_p, psf_bank, scenes)
    w1 = jnp.pad(conv_in.transpose(0, 2, 3, 1), ((0, 0), (0, 0), (0, 0), (0, 5))).reshape(-1, 72)
    w2 = conv_out.transpose(0, 2, 3, 1).reshape(conv_out.shape[0], -1)
    return finish(col, w1, w2, waves, n)


def solution(mesh):
    in_specs = (
        P("tile", "wave", None),
        P("wave", "tile", None),
        P("wave", "tile", None),
        P("wave", "tile"),
        P("wave", "tile"),
        P("wave", "tile"),
        P(None, "wave", None),
        P("tile", None, None),
        P(),
        P(),
        P(),
    )
    out_specs = P("wave", None, "tile", None)
    return jax.shard_map(
        per_device, mesh=mesh, in_specs=in_specs, out_specs=out_specs, check_vma=False
    )
```

```python
import functools

import jax
import jax.numpy as jnp
from jax import lax
from jax.experimental import pallas as pl
from jax.experimental.pallas import tpu as pltpu
from jax.sharding import PartitionSpec as P

ROWS = 16
W = 128
WIN = 4
K = 31
RAD = K // 2
PITCH = 32
DEPTH = ROWS * PITCH
MESH = pl.DeviceIdType.MESH
F32 = jnp.float32
BF16 = jnp.bfloat16


def pack_kernel(n, cap, scenes, tile_ref, count_ref, scene_ref, row_ref, index_ref, energy_ref, spot_ref,
                out_e, out_p, out_m, places, used):
    blocks = energy_ref.shape[0]
    halves = out_p.shape[1]
    out_e[...] = jnp.zeros_like(out_e)
    places[...] = jnp.full_like(places, 1023)
    for t in range(n):
        used[t] = 0
        for j in range(cap):
            out_m[t, j] = 0
        for s in range(scenes):
            out_m[t, 64 + s] = index_ref[0, s]
    lane = lax.broadcasted_iota(jnp.int32, (1, W), 1)

    def place(i, carry):
        t = tile_ref[0, i]
        j = used[t]
        used[t] = j + 1
        out_m[t, j] = scene_ref[0, i] * ROWS + row_ref[0, i]
        out_e[t, j] = energy_ref[i]
        places[t, pl.ds(j, 1), :] = jnp.where(lane < count_ref[0, i], spot_ref[0, pl.ds(i, 1), :], 1023)
        return carry

    lax.fori_loop(0, blocks, place, 0, unroll=8)
    step = cap // 2
    if halves == step:
        for t in range(n):
            out_p[t] = places[t, :step] + places[t, step:] * 65536
    else:
        out_p[...] = places[...]


def pack(block_tile, block_count, block_scene, block_row, psf_index, energy, spot, n):
    blocks, bands, lanes = energy.shape
    cap = 2 * blocks // n
    halves = cap // 2 if cap % 16 == 0 else cap
    scenes = psf_index.shape[1]
    vmem = pl.BlockSpec(memory_space=pltpu.VMEM)
    smem = pl.BlockSpec(memory_space=pltpu.SMEM)
    return pl.pallas_call(
        functools.partial(pack_kernel, n, cap, scenes),
        out_shape=(
            jax.ShapeDtypeStruct((n, cap, bands, lanes), energy.dtype),
            jax.ShapeDtypeStruct((n, halves, lanes), jnp.int32),
            jax.ShapeDtypeStruct((n, lanes), jnp.int32),
        ),
        in_specs=[smem] * 5 + [vmem] * 2,
        out_specs=(vmem, vmem, smem),
        scratch_shapes=[pltpu.VMEM((n, cap, lanes), jnp.int32), pltpu.SMEM((n,), jnp.int32)],
        compiler_params=pltpu.CompilerParams(vmem_limit_bytes=63 * 2**20),
        name="pack",
    )(block_tile, block_count, block_scene, block_row, psf_index, energy, spot)


def dispatch_kernel(n, scenes, bands, send_e, send_p, send_m, bank_hbm, got_e, got_p, got_m, toeplitz,
                    bank_ref, index_ref, kpad, amat, send_sem, recv_sem, local_sem):
    wave = lax.axis_index("wave")
    me = lax.axis_index("tile")
    load_bank = pltpu.make_async_copy(bank_hbm, bank_ref, local_sem.at[3])
    load_bank.start()
    barrier = pltpu.get_barrier_semaphore()

    @pl.loop(1, n)
    def _(d):
        pl.semaphore_signal(barrier, inc=1, device_id=(wave, lax.rem(me + d, n)), device_id_type=MESH)

    arrays = ((send_e, got_e), (send_p, got_p), (send_m, got_m))

    def copy_of(k, d):
        peer = lax.rem(me + d, n)
        src, dst = arrays[k]
        return pltpu.make_async_remote_copy(
            src_ref=src.at[peer], dst_ref=dst.at[me], send_sem=send_sem.at[k, d],
            recv_sem=recv_sem.at[k, d], device_id=(wave, peer), device_id_type=MESH)

    own = [pltpu.make_async_copy(src.at[me], dst.at[me], local_sem.at[k]) for k, (src, dst) in enumerate(arrays)]
    for copy in own:
        copy.start()
    pl.semaphore_wait(barrier, n - 1)

    @pl.loop(1, n)
    def _(d):
        copy_of(2, d).start()

    @pl.loop(1, n)
    def _(d):
        copy_of(0, d).start()
        copy_of(1, d).start()

    for copy in own:
        copy.wait()

    @pl.loop(1, n)
    def _(d):
        copy_of(2, d).wait()

    fetch = pltpu.make_async_copy(got_m, index_ref, local_sem.at[4])
    fetch.start()
    fetch.wait()
    load_bank.wait()

    lane = lax.broadcasted_iota(jnp.int32, (bands, W), 1)
    kpad[...] = jnp.zeros_like(kpad)

    def scene_step(s, carry):
        for part in range(3):
            other = jnp.clip(me + part - 1, 0, n - 1)
            flat = bank_ref[index_ref[other, 0, 64 + s]]
            flat = jnp.concatenate([flat, jnp.zeros((bands, 1024 + W - K * K), F32)], axis=1)
            for g in range(8):
                cell = jnp.zeros((bands, W), F32)
                for q in range(4):
                    u = 4 * g + q
                    if u >= K:
                        continue
                    base = K * u // W * W
                    shift = (PITCH * q - (K * u - base)) % (2 * W)
                    piece = flat[:, base:base + 2 * W]
                    if shift:
                        piece = pltpu.roll(piece, shift, 1)
                    hit = (lane >= PITCH * q) & (lane < PITCH * q + K)
                    cell = jnp.where(hit, piece[:, :W], cell)
                kpad[:, 512 + g * W:512 + (g + 1) * W] = cell
            for j in range(ROWS):
                start = 512 + PITCH * (RAD - j + ROWS * (1 - part))
                base = start // W * W
                off = start - base
                piece = kpad[:, base:base + DEPTH + W]
                if off:
                    piece = pltpu.roll(piece, DEPTH + W - off, 1)
                for c4 in range(DEPTH // W):
                    amat[c4, pl.ds(part * ROWS + j, bands, stride=3 * ROWS), :] = (
                        piece[:, c4 * W:(c4 + 1) * W])
        for b in range(bands):
            for c4 in range(DEPTH // W):
                toeplitz[s, b, :, c4 * W:(c4 + 1) * W] = (
                    amat[c4, b * 3 * ROWS:(b + 1) * 3 * ROWS, :].astype(BF16))
        return carry

    lax.fori_loop(0, scenes, scene_step, 0)

    @pl.loop(1, n)
    def _(d):
        copy_of(0, d).wait()
        copy_of(1, d).wait()


def dispatch(energy, pos, meta, bank, scenes):
    n, cap, bands, lanes = energy.shape
    vmem = pl.BlockSpec(memory_space=pltpu.VMEM)
    hbm = pl.BlockSpec(memory_space=pl.ANY)
    return pl.pallas_call(
        functools.partial(dispatch_kernel, n, scenes, bands),
        out_shape=(
            jax.ShapeDtypeStruct(energy.shape, energy.dtype),
            jax.ShapeDtypeStruct(pos.shape, pos.dtype),
            jax.ShapeDtypeStruct(meta.shape, meta.dtype),
            jax.ShapeDtypeStruct((scenes, bands, 3 * ROWS, DEPTH), BF16),
        ),
        in_specs=[hbm] * 4,
        out_specs=(hbm, hbm, hbm, vmem),
        scratch_shapes=[
            pltpu.VMEM(bank.shape, F32),
            pltpu.SMEM(meta.shape, jnp.int32),
            pltpu.VMEM((bands, 2176), F32),
            pltpu.VMEM((DEPTH // W, bands * 3 * ROWS, W), F32),
            pltpu.SemaphoreType.DMA((3, n)),
            pltpu.SemaphoreType.DMA((3, n)),
            pltpu.SemaphoreType.DMA((5,)),
        ],
        compiler_params=pltpu.CompilerParams(
            collective_id=0, has_side_effects=True, vmem_limit_bytes=63 * 2**20),
        name="dispatch",
    )(energy, pos, meta, bank)


def splat_kernel(n, cap, bands, meta_ref, energy_ref, pos_ref, acc):
    group = 8
    halves = pos_ref.shape[1]
    acc[...] = jnp.zeros_like(acc)
    xs = lax.broadcasted_iota(jnp.int32, (W, W), 0)

    def splat_source(d, carry):
        @pl.loop(0, cap // group)
        def _(g):
            windows = []
            for k in range(group):
                j = g * group + k
                if halves == cap:
                    pos = pos_ref[d, pl.ds(j, 1), :]
                else:
                    pos = pos_ref[d, pl.ds(lax.rem(j, halves), 1), :]
                    pos = jnp.where(j < halves, pos & 65535, lax.shift_right_arithmetic(pos, 16))
                row = lax.shift_right_arithmetic(pos, 7)
                col = (W - 1) - (pos & (W - 1))
                onehot = jnp.where(xs == col, 1.0, 0.0).astype(BF16)
                energy = energy_ref[d, j].astype(F32)
                parts = [jnp.where(row == r, energy, 0.0) for r in range(WIN)]
                lhs = jnp.concatenate(parts, axis=0).astype(BF16)
                windows.append(lax.dot_general(
                    lhs, onehot, (((1,), (1,)), ((), ())), preferred_element_type=F32))
            for k in range(group):
                base = pl.multiple_of(meta_ref[d, g * group + k] * bands, bands)
                acc[pl.ds(base, WIN * bands), :] += windows[k]
        return carry

    lax.fori_loop(0, n, splat_source, 0)


def splat(meta, energy, pos, scenes):
    n, cap, bands, lanes = energy.shape
    vmem = pl.BlockSpec(memory_space=pltpu.VMEM)
    smem = pl.BlockSpec(memory_space=pltpu.SMEM)
    return pl.pallas_call(
        functools.partial(splat_kernel, n, cap, bands),
        out_shape=jax.ShapeDtypeStruct((scenes * ROWS * bands, W), F32),
        in_specs=[smem, vmem, vmem],
        out_specs=vmem,
        compiler_params=pltpu.CompilerParams(vmem_limit_bytes=63 * 2**20),
        name="splat",
    )(meta, energy, pos)


def finish_kernel(waves, n, resp_ref, acc, toeplitz, w1_ref, w2_ref, out_ref, col_ref, got, mine, rim, sens, hid, outs,
                  send_sem, recv_sem, rim_send, rim_recv):
    wave = lax.axis_index("wave")
    me = lax.axis_index("tile")
    has_up = me > 0
    has_down = me < n - 1
    barrier = pltpu.get_barrier_semaphore()

    def guarded(part, body):
        if part == 0:
            pl.when(has_up)(body)
        elif part == 2:
            pl.when(has_down)(body)
        else:
            body()

    todo = [(dw, part) for dw in range(waves) for part in range(3) if (dw, part) != (0, 1)]
    for dw, part in todo:
        def greet(dw=dw, part=part):
            pl.semaphore_signal(barrier, inc=1,
                                device_id=(lax.rem(wave + dw, waves), me + part - 1), device_id_type=MESH)
        guarded(part, greet)
    sides = jnp.where(has_up, 1, 0) + jnp.where(has_down, 1, 0)
    pl.semaphore_wait(barrier, waves - 1 + waves * sides)

    def copy_of(dw, part):
        scene = lax.rem(wave + dw, waves)
        return pltpu.make_async_remote_copy(
            src_ref=col_ref.at[scene, part], dst_ref=got.at[dw, part],
            send_sem=send_sem.at[dw, part], recv_sem=recv_sem.at[dw, part],
            device_id=(scene, me + part - 1), device_id_type=MESH)

    bands = toeplitz.shape[1]
    shift_v = lax.broadcasted_iota(jnp.int32, (PITCH, W), 0)
    from_x = lax.broadcasted_iota(jnp.int32, (PITCH, W), 1) - shift_v + RAD
    keep = (from_x >= 0) & (from_x < W) & (shift_v < K)

    def scene_step(i, carry):
        dw = lax.rem(i + 1, waves)
        s = lax.rem(wave + dw, waves)
        colours = [jnp.zeros((3 * ROWS, W), F32) for _ in range(3)]
        for b in range(bands):
            rows = []
            for r in range(ROWS):
                line = acc[pl.ds((s * ROWS + r) * bands + b, 1), :]
                wide = jnp.broadcast_to(line, (PITCH, W))
                wide = pltpu.roll(wide, W - RAD, 1, stride=1, stride_axis=0)
                rows.append(jnp.where(keep, wide, 0.0).astype(BF16))
            rhs = jnp.concatenate(rows, axis=0)
            blurred = jnp.dot(toeplitz[s, b], rhs, preferred_element_type=F32)
            for c in range(3):
                colours[c] = colours[c] + resp_ref[c, wave * bands + b] * blurred
        for part in range(3):
            for c in range(3):
                col_ref[s, part, c] = colours[c][part * ROWS:(part + 1) * ROWS]
        pl.when(has_up)(lambda: copy_of(dw, 0).start())
        pl.when(dw > 0)(lambda: copy_of(dw, 1).start())
        pl.when(has_down)(lambda: copy_of(dw, 2).start())
        return carry

    lax.fori_loop(0, waves, scene_step, 0)

    @pl.when(jnp.logical_not(has_down))
    def _():
        for dw in range(waves):
            got[dw, 0] = jnp.zeros(got.shape[2:], F32)
        rim[1] = jnp.zeros(rim.shape[1:], F32)

    @pl.when(jnp.logical_not(has_up))
    def _():
        for dw in range(waves):
            got[dw, 2] = jnp.zeros(got.shape[2:], F32)
        rim[0] = jnp.zeros(rim.shape[1:], F32)

    for dw, part in todo:
        guarded(2 - part, lambda dw=dw, part=part: copy_of(dw, part).wait_recv())
    total = col_ref[wave, 1]
    for dw, part in todo:
        total = total + got[dw, part]
    sensor = total.astype(BF16)
    flip_r = lax.broadcasted_iota(jnp.int32, (W, W), 0)
    flip_c = lax.broadcasted_iota(jnp.int32, (W, W), 1)
    mirror = jnp.where(flip_r + flip_c == W - 1, 1.0, 0.0).astype(BF16)
    plain = jnp.dot(sensor.reshape(3 * ROWS, W), mirror, preferred_element_type=F32)
    mine[...] = plain.reshape(3, ROWS, W)

    def to_down():
        return pltpu.make_async_remote_copy(
            src_ref=mine.at[:, pl.ds(8, 8)], dst_ref=rim.at[0], send_sem=rim_send.at[0],
            recv_sem=rim_recv.at[0], device_id=(wave, me + 1), device_id_type=MESH)

    def to_up():
        return pltpu.make_async_remote_copy(
            src_ref=mine.at[:, pl.ds(0, 8)], dst_ref=rim.at[1], send_sem=rim_send.at[1],
            recv_sem=rim_recv.at[1], device_id=(wave, me - 1), device_id_type=MESH)

    pl.when(has_down)(lambda: to_down().start())
    pl.when(has_up)(lambda: to_up().start())

    sens[...] = jnp.zeros_like(sens)
    for c in range(3):
        sens[pl.ds(2 * 8 + c, ROWS, stride=8), :] = plain[c * ROWS:(c + 1) * ROWS]
    pl.when(has_up)(lambda: to_down().wait_recv())
    pl.when(has_down)(lambda: to_up().wait_recv())
    for c in range(3):
        for k in range(2):
            sens[pl.ds(k * 8 + c, 1), :] = rim[0, c, 6 + k:7 + k]
            sens[pl.ds((ROWS + 2 + k) * 8 + c, 1), :] = rim[1, c, k:k + 1]

    def shifted(values):
        xs = lax.broadcasted_iota(jnp.int32, values.shape, 1)
        left = jnp.where(xs == 0, 0.0, pltpu.roll(values, 1, 1))
        right = jnp.where(xs == W - 1, 0.0, pltpu.roll(values, W - 1, 1))
        return left, values, right

    spread = jnp.concatenate(
        [jnp.concatenate(shifted(sens[y * 8:(y + 1) * 8, :]), axis=0) for y in range(ROWS + 4)], axis=0
    )
    w1 = w1_ref[...]
    for y in range(ROWS + 2):
        rhs = spread[y * 24:(y + 3) * 24].astype(BF16)
        value = jnp.dot(w1, rhs, preferred_element_type=F32)
        value = value / (1.0 + jnp.exp(-value))
        if y == 0:
            value = jnp.where(has_up, value, 0.0)
        if y == ROWS + 1:
            value = jnp.where(has_down, value, 0.0)
        hid[y] = jnp.concatenate(shifted(value), axis=0).astype(BF16)
    w2 = w2_ref[...]
    channels = w2.shape[0]
    for y in range(ROWS):
        rhs = hid[y:y + 3].reshape(9 * channels, W)
        outs[pl.ds(y, channels, stride=ROWS), :] = jnp.dot(w2, rhs, preferred_element_type=F32)
    out_ref[0] = outs[...].reshape(channels, ROWS, W).astype(BF16)

    for dw, part in todo:
        guarded(part, lambda dw=dw, part=part: copy_of(dw, part).wait_send())
    pl.when(has_down)(lambda: to_down().wait_send())
    pl.when(has_up)(lambda: to_up().wait_send())


def finish(response, acc, toeplitz, w1, w2, waves, n):
    channels = w2.shape[0]
    vmem = pl.BlockSpec(memory_space=pltpu.VMEM)
    return pl.pallas_call(
        functools.partial(finish_kernel, waves, n),
        out_shape=jax.ShapeDtypeStruct((1, channels, ROWS, W), BF16),
        in_specs=[pl.BlockSpec(memory_space=pltpu.SMEM)] + [vmem] * 4,
        out_specs=vmem,
        scratch_shapes=[
            pltpu.VMEM((waves, 3, 3, ROWS, W), F32),
            pltpu.VMEM((waves, 3, 3, ROWS, W), F32),
            pltpu.VMEM((3, ROWS, W), F32),
            pltpu.VMEM((2, 3, 8, W), F32),
            pltpu.VMEM(((ROWS + 4) * 8, W), F32),
            pltpu.VMEM((ROWS + 2, 3 * channels, W), BF16),
            pltpu.VMEM((channels * ROWS, W), F32),
            pltpu.SemaphoreType.DMA((waves, 3)),
            pltpu.SemaphoreType.DMA((waves, 3)),
            pltpu.SemaphoreType.DMA((2,)),
            pltpu.SemaphoreType.DMA((2,)),
        ],
        compiler_params=pltpu.CompilerParams(
            collective_id=1, has_side_effects=True, vmem_limit_bytes=63 * 2**20),
        name="finish",
    )(response, acc, toeplitz, w1, w2)


def per_device(hit_energy, hit_spot, block_tile, block_count, block_scene, block_row, psf_bank,
               psf_index, response, conv_in, conv_out):
    n = lax.axis_size("tile")
    waves = lax.axis_size("wave")
    scenes = psf_index.shape[1]
    blocks = hit_energy.shape[0]
    send_e, send_p, send_m = pack(
        block_tile.reshape(1, blocks), block_count, block_scene, block_row, psf_index.reshape(1, scenes),
        hit_energy, hit_spot, n)
    got_e, got_p, got_m, toeplitz = dispatch(send_e, send_p, send_m[:, None, :], psf_bank, scenes)
    acc = splat(got_m[:, 0, :], got_e, got_p, scenes)
    w1 = jnp.pad(conv_in.transpose(0, 2, 3, 1), ((0, 0), (0, 0), (0, 0), (0, 5))).reshape(-1, 72)
    w2 = conv_out.transpose(0, 2, 3, 1).reshape(conv_out.shape[0], -1)
    return finish(response.T, acc, toeplitz, w1, w2, waves, n)


def solution(mesh):
    in_specs = (
        P("tile", "wave", None),
        P("wave", "tile", None),
        P("wave", "tile", None),
        P("wave", "tile"),
        P("wave", "tile"),
        P("wave", "tile"),
        P(None, "wave", None),
        P("tile", None, None),
        P(),
        P(),
        P(),
    )
    out_specs = P("wave", None, "tile", None)
    return jax.shard_map(
        per_device, mesh=mesh, in_specs=in_specs, out_specs=out_specs, check_vma=False
    )
```

```python
import functools
import math

import jax
import jax.numpy as jnp
from jax import lax
from jax.experimental import pallas as pl
from jax.experimental.pallas import tpu as pltpu
from jax.sharding import PartitionSpec as P

ROWS = 16
W = 128
WIN = 4
K = 31
RAD = K // 2
PITCH = 32
DEPTH = ROWS * PITCH
MESH = pl.DeviceIdType.MESH
F32 = jnp.float32
BF16 = jnp.bfloat16


def pack_kernel(n, cap, scenes, tile_ref, count_ref, scene_ref, row_ref, index_ref, energy_ref, spot_ref,
                out_e, out_p, out_m, places, used):
    blocks = energy_ref.shape[0]
    halves = out_p.shape[1]
    out_e[...] = jnp.zeros_like(out_e)
    places[...] = jnp.full_like(places, 1023)
    for t in range(n):
        used[t] = 0
        for j in range(cap):
            out_m[t, j] = 0
        for s in range(scenes):
            out_m[t, 64 + s] = index_ref[0, s]
    lane = lax.broadcasted_iota(jnp.int32, (1, W), 1)

    def place(i, carry):
        t = tile_ref[0, i]
        j = used[t]
        used[t] = j + 1
        out_m[t, j] = scene_ref[0, i] * ROWS + row_ref[0, i]
        out_e[t, j] = energy_ref[i]
        places[t, pl.ds(j, 1), :] = jnp.where(lane < count_ref[0, i], spot_ref[0, pl.ds(i, 1), :], 1023)
        return carry

    lax.fori_loop(0, blocks, place, 0, unroll=8)
    step = cap // 2
    if halves == step:
        for t in range(n):
            out_p[t] = places[t, :step] + places[t, step:] * 65536
    else:
        out_p[...] = places[...]


def pack(block_tile, block_count, block_scene, block_row, psf_index, energy, spot, n):
    blocks, bands, lanes = energy.shape
    cap = 2 * blocks // n
    halves = cap // 2 if cap % 16 == 0 else cap
    scenes = psf_index.shape[1]
    vmem = pl.BlockSpec(memory_space=pltpu.VMEM)
    smem = pl.BlockSpec(memory_space=pltpu.SMEM)
    return pl.pallas_call(
        functools.partial(pack_kernel, n, cap, scenes),
        out_shape=(
            jax.ShapeDtypeStruct((n, cap, bands, lanes), energy.dtype),
            jax.ShapeDtypeStruct((n, halves, lanes), jnp.int32),
            jax.ShapeDtypeStruct((n, lanes), jnp.int32),
        ),
        in_specs=[smem] * 5 + [vmem] * 2,
        out_specs=(vmem, vmem, smem),
        scratch_shapes=[pltpu.VMEM((n, cap, lanes), jnp.int32), pltpu.SMEM((n,), jnp.int32)],
        compiler_params=pltpu.CompilerParams(vmem_limit_bytes=63 * 2**20),
        name="pack",
    )(block_tile, block_count, block_scene, block_row, psf_index, energy, spot)


def dispatch_kernel(n, scenes, bands, send_e, send_p, send_m, bank_hbm, got_e, got_p, got_m, toeplitz,
                    bank_ref, index_ref, kpad, amat, send_sem, recv_sem, local_sem):
    wave = lax.axis_index("wave")
    me = lax.axis_index("tile")
    load_bank = pltpu.make_async_copy(bank_hbm, bank_ref, local_sem.at[3])
    load_bank.start()
    barrier = pltpu.get_barrier_semaphore()

    @pl.loop(1, n)
    def _(d):
        pl.semaphore_signal(barrier, inc=1, device_id=(wave, lax.rem(me + d, n)), device_id_type=MESH)

    arrays = ((send_e, got_e), (send_p, got_p), (send_m, got_m))

    def copy_of(k, d):
        peer = lax.rem(me + d, n)
        src, dst = arrays[k]
        return pltpu.make_async_remote_copy(
            src_ref=src.at[peer], dst_ref=dst.at[me], send_sem=send_sem.at[k, d],
            recv_sem=recv_sem.at[k, d], device_id=(wave, peer), device_id_type=MESH)

    own = [pltpu.make_async_copy(src.at[me], dst.at[me], local_sem.at[k]) for k, (src, dst) in enumerate(arrays)]
    for copy in own:
        copy.start()
    pl.semaphore_wait(barrier, n - 1)

    @pl.loop(1, n)
    def _(d):
        copy_of(2, d).start()

    @pl.loop(1, n)
    def _(d):
        copy_of(0, d).start()
        copy_of(1, d).start()

    for copy in own:
        copy.wait()

    @pl.loop(1, n)
    def _(d):
        copy_of(2, d).wait()

    fetch = pltpu.make_async_copy(got_m, index_ref, local_sem.at[4])
    fetch.start()
    fetch.wait()
    load_bank.wait()

    lane = lax.broadcasted_iota(jnp.int32, (bands, W), 1)
    kpad[...] = jnp.zeros_like(kpad)

    def scene_step(s, carry):
        for part in range(3):
            other = jnp.clip(me + part - 1, 0, n - 1)
            flat = bank_ref[index_ref[other, 0, 64 + s]]
            flat = jnp.concatenate([flat, jnp.zeros((bands, 1024 + W - K * K), F32)], axis=1)
            for g in range(8):
                cell = jnp.zeros((bands, W), F32)
                for q in range(4):
                    u = 4 * g + q
                    if u >= K:
                        continue
                    base = K * u // W * W
                    shift = (PITCH * q - (K * u - base)) % (2 * W)
                    piece = flat[:, base:base + 2 * W]
                    if shift:
                        piece = pltpu.roll(piece, shift, 1)
                    hit = (lane >= PITCH * q) & (lane < PITCH * q + K)
                    cell = jnp.where(hit, piece[:, :W], cell)
                kpad[:, 512 + g * W:512 + (g + 1) * W] = cell
            for j in range(ROWS):
                start = 512 + PITCH * (RAD - j + ROWS * (1 - part))
                base = start // W * W
                off = start - base
                piece = kpad[:, base:base + DEPTH + W]
                if off:
                    piece = pltpu.roll(piece, DEPTH + W - off, 1)
                for c4 in range(DEPTH // W):
                    amat[c4, pl.ds(part * ROWS + j, bands, stride=3 * ROWS), :] = (
                        piece[:, c4 * W:(c4 + 1) * W])
        for b in range(bands):
            for c4 in range(DEPTH // W):
                toeplitz[s, b, :, c4 * W:(c4 + 1) * W] = (
                    amat[c4, b * 3 * ROWS:(b + 1) * 3 * ROWS, :].astype(BF16))
        return carry

    lax.fori_loop(0, scenes, scene_step, 0)

    @pl.loop(1, n)
    def _(d):
        copy_of(0, d).wait()
        copy_of(1, d).wait()


def dispatch(energy, pos, meta, bank, scenes):
    n, cap, bands, lanes = energy.shape
    vmem = pl.BlockSpec(memory_space=pltpu.VMEM)
    hbm = pl.BlockSpec(memory_space=pl.ANY)
    return pl.pallas_call(
        functools.partial(dispatch_kernel, n, scenes, bands),
        out_shape=(
            jax.ShapeDtypeStruct(energy.shape, energy.dtype),
            jax.ShapeDtypeStruct(pos.shape, pos.dtype),
            jax.ShapeDtypeStruct(meta.shape, meta.dtype),
            jax.ShapeDtypeStruct((scenes, bands, 3 * ROWS, DEPTH), BF16),
        ),
        in_specs=[hbm] * 4,
        out_specs=(hbm, hbm, hbm, vmem),
        scratch_shapes=[
            pltpu.VMEM(bank.shape, F32),
            pltpu.SMEM(meta.shape, jnp.int32),
            pltpu.VMEM((bands, 2176), F32),
            pltpu.VMEM((DEPTH // W, bands * 3 * ROWS, W), F32),
            pltpu.SemaphoreType.DMA((3, n)),
            pltpu.SemaphoreType.DMA((3, n)),
            pltpu.SemaphoreType.DMA((5,)),
        ],
        compiler_params=pltpu.CompilerParams(
            collective_id=0, has_side_effects=True, vmem_limit_bytes=63 * 2**20),
        name="dispatch",
    )(energy, pos, meta, bank)


def splat_kernel(n, cap, bands, meta_ref, energy_ref, pos_ref, acc):
    group = math.gcd(cap, 32)
    halves = pos_ref.shape[1]
    acc[...] = jnp.zeros_like(acc)
    xs = lax.broadcasted_iota(jnp.int32, (W, W), 0)

    def splat_source(d, carry):
        @pl.loop(0, cap // group)
        def _(g):
            windows = []
            for k in range(group):
                j = g * group + k
                if halves == cap:
                    pos = pos_ref[d, pl.ds(j, 1), :]
                else:
                    pos = pos_ref[d, pl.ds(lax.rem(j, halves), 1), :]
                    pos = jnp.where(j < halves, pos & 65535, lax.shift_right_arithmetic(pos, 16))
                row = lax.shift_right_arithmetic(pos, 7)
                col = (W - 1) - (pos & (W - 1))
                onehot = jnp.where(xs == col, 1.0, 0.0).astype(BF16)
                energy = energy_ref[d, j].astype(F32)
                parts = [jnp.where(row == r, energy, 0.0) for r in range(WIN)]
                lhs = jnp.concatenate(parts, axis=0).astype(BF16)
                windows.append(lax.dot_general(
                    lhs, onehot, (((1,), (1,)), ((), ())), preferred_element_type=F32))
            for k in range(group):
                base = pl.multiple_of(meta_ref[d, g * group + k] * bands, bands)
                acc[pl.ds(base, WIN * bands), :] += windows[k]
        return carry

    lax.fori_loop(0, n, splat_source, 0)


def splat(meta, energy, pos, scenes):
    n, cap, bands, lanes = energy.shape
    vmem = pl.BlockSpec(memory_space=pltpu.VMEM)
    smem = pl.BlockSpec(memory_space=pltpu.SMEM)
    return pl.pallas_call(
        functools.partial(splat_kernel, n, cap, bands),
        out_shape=jax.ShapeDtypeStruct((scenes * ROWS * bands, W), F32),
        in_specs=[smem, vmem, vmem],
        out_specs=vmem,
        compiler_params=pltpu.CompilerParams(vmem_limit_bytes=63 * 2**20),
        name="splat",
    )(meta, energy, pos)


def finish_kernel(waves, n, resp_ref, acc, toeplitz, w1_ref, w2_ref, out_ref, col_ref, got, mine, rim, sens, hid, outs,
                  send_sem, recv_sem, rim_send, rim_recv):
    wave = lax.axis_index("wave")
    me = lax.axis_index("tile")
    has_up = me > 0
    has_down = me < n - 1
    barrier = pltpu.get_barrier_semaphore()

    def guarded(part, body):
        if part == 0:
            pl.when(has_up)(body)
        elif part == 2:
            pl.when(has_down)(body)
        else:
            body()

    todo = [(dw, part) for dw in range(waves) for part in range(3) if (dw, part) != (0, 1)]
    for dw, part in todo:
        def greet(dw=dw, part=part):
            pl.semaphore_signal(barrier, inc=1,
                                device_id=(lax.rem(wave + dw, waves), me + part - 1), device_id_type=MESH)
        guarded(part, greet)
    sides = jnp.where(has_up, 1, 0) + jnp.where(has_down, 1, 0)
    pl.semaphore_wait(barrier, waves - 1 + waves * sides)

    def copy_of(dw, part):
        scene = lax.rem(wave + dw, waves)
        return pltpu.make_async_remote_copy(
            src_ref=col_ref.at[scene, part], dst_ref=got.at[dw, part],
            send_sem=send_sem.at[dw, part], recv_sem=recv_sem.at[dw, part],
            device_id=(scene, me + part - 1), device_id_type=MESH)

    bands = toeplitz.shape[1]
    shift_v = lax.broadcasted_iota(jnp.int32, (PITCH, W), 0)
    from_x = lax.broadcasted_iota(jnp.int32, (PITCH, W), 1) - shift_v + RAD
    keep = (from_x >= 0) & (from_x < W) & (shift_v < K)

    def scene_step(i, carry):
        dw = lax.rem(i + 1, waves)
        s = lax.rem(wave + dw, waves)
        colours = [jnp.zeros((3 * ROWS, W), F32) for _ in range(3)]
        for b in range(bands):
            rows = []
            for r in range(ROWS):
                line = acc[pl.ds((s * ROWS + r) * bands + b, 1), :]
                wide = jnp.broadcast_to(line, (PITCH, W))
                wide = pltpu.roll(wide, W - RAD, 1, stride=1, stride_axis=0)
                rows.append(jnp.where(keep, wide, 0.0).astype(BF16))
            rhs = jnp.concatenate(rows, axis=0)
            blurred = jnp.dot(toeplitz[s, b], rhs, preferred_element_type=F32)
            for c in range(3):
                colours[c] = colours[c] + resp_ref[c, wave * bands + b] * blurred
        for part in range(3):
            for c in range(3):
                col_ref[s, part, c] = colours[c][part * ROWS:(part + 1) * ROWS]
        pl.when(has_up)(lambda: copy_of(dw, 0).start())
        pl.when(dw > 0)(lambda: copy_of(dw, 1).start())
        pl.when(has_down)(lambda: copy_of(dw, 2).start())
        return carry

    lax.fori_loop(0, waves, scene_step, 0)

    @pl.when(jnp.logical_not(has_down))
    def _():
        for dw in range(waves):
            got[dw, 0] = jnp.zeros(got.shape[2:], F32)
        rim[1] = jnp.zeros(rim.shape[1:], F32)

    @pl.when(jnp.logical_not(has_up))
    def _():
        for dw in range(waves):
            got[dw, 2] = jnp.zeros(got.shape[2:], F32)
        rim[0] = jnp.zeros(rim.shape[1:], F32)

    for dw, part in todo:
        guarded(2 - part, lambda dw=dw, part=part: copy_of(dw, part).wait_recv())
    total = col_ref[wave, 1]
    for dw, part in todo:
        total = total + got[dw, part]
    sensor = total.astype(BF16)
    flip_r = lax.broadcasted_iota(jnp.int32, (W, W), 0)
    flip_c = lax.broadcasted_iota(jnp.int32, (W, W), 1)
    mirror = jnp.where(flip_r + flip_c == W - 1, 1.0, 0.0).astype(BF16)
    plain = jnp.dot(sensor.reshape(3 * ROWS, W), mirror, preferred_element_type=F32)
    mine[...] = plain.reshape(3, ROWS, W)

    def to_down():
        return pltpu.make_async_remote_copy(
            src_ref=mine.at[:, pl.ds(8, 8)], dst_ref=rim.at[0], send_sem=rim_send.at[0],
            recv_sem=rim_recv.at[0], device_id=(wave, me + 1), device_id_type=MESH)

    def to_up():
        return pltpu.make_async_remote_copy(
            src_ref=mine.at[:, pl.ds(0, 8)], dst_ref=rim.at[1], send_sem=rim_send.at[1],
            recv_sem=rim_recv.at[1], device_id=(wave, me - 1), device_id_type=MESH)

    pl.when(has_down)(lambda: to_down().start())
    pl.when(has_up)(lambda: to_up().start())

    sens[...] = jnp.zeros_like(sens)
    for c in range(3):
        sens[pl.ds(2 * 8 + c, ROWS, stride=8), :] = plain[c * ROWS:(c + 1) * ROWS]
    pl.when(has_up)(lambda: to_down().wait_recv())
    pl.when(has_down)(lambda: to_up().wait_recv())
    for c in range(3):
        for k in range(2):
            sens[pl.ds(k * 8 + c, 1), :] = rim[0, c, 6 + k:7 + k]
            sens[pl.ds((ROWS + 2 + k) * 8 + c, 1), :] = rim[1, c, k:k + 1]

    def shifted(values):
        xs = lax.broadcasted_iota(jnp.int32, values.shape, 1)
        left = jnp.where(xs == 0, 0.0, pltpu.roll(values, 1, 1))
        right = jnp.where(xs == W - 1, 0.0, pltpu.roll(values, W - 1, 1))
        return left, values, right

    spread = jnp.concatenate(
        [jnp.concatenate(shifted(sens[y * 8:(y + 1) * 8, :]), axis=0) for y in range(ROWS + 4)], axis=0
    )
    w1 = w1_ref[...]
    for y in range(ROWS + 2):
        rhs = spread[y * 24:(y + 3) * 24].astype(BF16)
        value = jnp.dot(w1, rhs, preferred_element_type=F32)
        value = value / (1.0 + jnp.exp(-value))
        if y == 0:
            value = jnp.where(has_up, value, 0.0)
        if y == ROWS + 1:
            value = jnp.where(has_down, value, 0.0)
        hid[y] = jnp.concatenate(shifted(value), axis=0).astype(BF16)
    w2 = w2_ref[...]
    channels = w2.shape[0]
    for y in range(ROWS):
        rhs = hid[y:y + 3].reshape(9 * channels, W)
        outs[pl.ds(y, channels, stride=ROWS), :] = jnp.dot(w2, rhs, preferred_element_type=F32)
    out_ref[0] = outs[...].reshape(channels, ROWS, W).astype(BF16)

    for dw, part in todo:
        guarded(part, lambda dw=dw, part=part: copy_of(dw, part).wait_send())
    pl.when(has_down)(lambda: to_down().wait_send())
    pl.when(has_up)(lambda: to_up().wait_send())


def finish(response, acc, toeplitz, w1, w2, waves, n):
    channels = w2.shape[0]
    vmem = pl.BlockSpec(memory_space=pltpu.VMEM)
    return pl.pallas_call(
        functools.partial(finish_kernel, waves, n),
        out_shape=jax.ShapeDtypeStruct((1, channels, ROWS, W), BF16),
        in_specs=[pl.BlockSpec(memory_space=pltpu.SMEM)] + [vmem] * 4,
        out_specs=vmem,
        scratch_shapes=[
            pltpu.VMEM((waves, 3, 3, ROWS, W), F32),
            pltpu.VMEM((waves, 3, 3, ROWS, W), F32),
            pltpu.VMEM((3, ROWS, W), F32),
            pltpu.VMEM((2, 3, 8, W), F32),
            pltpu.VMEM(((ROWS + 4) * 8, W), F32),
            pltpu.VMEM((ROWS + 2, 3 * channels, W), BF16),
            pltpu.VMEM((channels * ROWS, W), F32),
            pltpu.SemaphoreType.DMA((waves, 3)),
            pltpu.SemaphoreType.DMA((waves, 3)),
            pltpu.SemaphoreType.DMA((2,)),
            pltpu.SemaphoreType.DMA((2,)),
        ],
        compiler_params=pltpu.CompilerParams(
            collective_id=1, has_side_effects=True, vmem_limit_bytes=63 * 2**20),
        name="finish",
    )(response, acc, toeplitz, w1, w2)


def per_device(hit_energy, hit_spot, block_tile, block_count, block_scene, block_row, psf_bank,
               psf_index, response, conv_in, conv_out):
    n = lax.axis_size("tile")
    waves = lax.axis_size("wave")
    scenes = psf_index.shape[1]
    blocks = hit_energy.shape[0]
    send_e, send_p, send_m = pack(
        block_tile.reshape(1, blocks), block_count, block_scene, block_row, psf_index.reshape(1, scenes),
        hit_energy, hit_spot, n)
    got_e, got_p, got_m, toeplitz = dispatch(send_e, send_p, send_m[:, None, :], psf_bank, scenes)
    acc = splat(got_m[:, 0, :], got_e, got_p, scenes)
    w1 = jnp.pad(conv_in.transpose(0, 2, 3, 1), ((0, 0), (0, 0), (0, 0), (0, 5))).reshape(-1, 72)
    w2 = conv_out.transpose(0, 2, 3, 1).reshape(conv_out.shape[0], -1)
    return finish(response.T, acc, toeplitz, w1, w2, waves, n)


def solution(mesh):
    in_specs = (
        P("tile", "wave", None),
        P("wave", "tile", None),
        P("wave", "tile", None),
        P("wave", "tile"),
        P("wave", "tile"),
        P("wave", "tile"),
        P(None, "wave", None),
        P("tile", None, None),
        P(),
        P(),
        P(),
    )
    out_specs = P("wave", None, "tile", None)
    return jax.shard_map(
        per_device, mesh=mesh, in_specs=in_specs, out_specs=out_specs, check_vma=False
    )
```
